32 devices in a mesh: seq: 16 (over z, y, x), head: 2 (over core).
Axes of the slice: x: 2, y: 2, z: 4, core: 2. Of those that a mesh axis runs over, the one named last changes fastest.
Arguments:
- tokens: bfloat16 [8192, 2048], P('seq'), may hold values from -6 to 6
- cotangent: bfloat16 [8192, 2048], P('seq'), may hold values from -6 to 6
- lengths: int32 [4], replicated, may hold values from 1 to 7936, 8192 in all
- order: int32 [4], replicated, may hold values from 0 to 3, each once
- norm1_gain: float32 [2048], replicated, may hold values from 0.5 to 1.5
- query_weight: bfloat16 [2048, 2048], P('seq', 'head'), may hold values from -0.125 to 0.125
- key_weight: bfloat16 [2048, 2048], P('seq', 'head'), may hold values from -0.125 to 0.125
- value_weight: bfloat16 [2048, 2048], P('seq', 'head'), may hold values from -0.125 to 0.125
- beta_weight: bfloat16 [2048, 16], P('seq', 'head'), may hold values from -0.125 to 0.125
- beta_bias: float32 [16], P('head'), may hold values from -8 to 0
- conv_query: float32 [4, 2048], P(None, 'head'), may hold values from -2.5 to 2.5
- conv_key: float32 [4, 2048], P(None, 'head'), may hold values from -2.5 to 2.5
- conv_value: float32 [4, 2048], P(None, 'head'), may hold values from -2.5 to 2.5
- out_norm_gain: float32 [128], replicated, may hold values from 0.5 to 1.5
- out_weight: bfloat16 [2048, 2048], P('head', 'seq'), may hold values from -0.125 to 0.125
- norm2_gain: float32 [2048], replicated, may hold values from 0.5 to 1.5
- gate_weight: bfloat16 [2048, 5632], P('seq', 'head'), may hold values from -0.125 to 0.125
- up_weight: bfloat16 [2048, 5632], P('seq', 'head'), may hold values from -0.125 to 0.125
- down_weight: bfloat16 [5632, 2048], P('head', 'seq'), may hold values from -0.078125 to 0.078125
Outputs:
- output: bfloat16 [8192, 2048], P('seq')
- input_grad: float32 [8192, 2048], P('seq')
- norm1_gain_grad: float32 [2048], replicated
- query_weight_grad: float32 [2048, 2048], P('seq', 'head')
- key_weight_grad: float32 [2048, 2048], P('seq', 'head')
- value_weight_grad: float32 [2048, 2048], P('seq', 'head')
- beta_weight_grad: float32 [2048, 16], P('seq', 'head')
- beta_bias_grad: float32 [16], P('head')
- conv_query_grad: float32 [4, 2048], P(None, 'head')
- conv_key_grad: float32 [4, 2048], P(None, 'head')
- conv_value_grad: float32 [4, 2048], P(None, 'head')
- out_norm_gain_grad: float32 [128], replicated
- out_weight_grad: float32 [2048, 2048], P('head', 'seq')
- norm2_gain_grad: float32 [2048], replicated
- gate_weight_grad: float32 [2048, 5632], P('seq', 'head')
- up_weight_grad: float32 [2048, 5632], P('seq', 'head')
- down_weight_grad: float32 [5632, 2048], P('head', 'seq')
The draws below stay inside these ranges and needn't reach their ends.
Inputs may be any that keep to these rules, and one draw needn't show every extreme that they name: `lengths`: they sum to 8192, and the longest has exactly 7936 tokens. `order`: each document number appears once.
All inputs are finite; a program needn't handle non-finite values.
Results may differ from the reference program's by a relative error of at most 0.01615.
Values may be sent and summed in bfloat16 or wider, within the bound.
No kernel may reach another device: no remote copies, remote signals or barrier semaphores. Data moves between devices by JAX's collectives and lax.ppermute only.
A program may use at most 320 MiB of HBM per device.

```python
import math
import jax
import jax.numpy as jnp
import numpy as np
from jax import lax

D = 2048
HEADS = 16
HEAD_DIM = 128
FF = 5632
SPAN = 64
KERNEL = 4
HD = 2048
TOKENS = 8192
MAXLEN = 7936
NSEQS = 4


def draw_beta_bias(key, part):
    key = jax.random.fold_in(key, 7)
    return jax.random.uniform(key, (HEADS,), jnp.float32, -8.0, 0.0)


def steps_of(key, shape, pieces, least, high):
    loudness, own = 1.0, jax.random.fold_in(key, 6)
    for position, shards_of in pieces:
        steps = jnp.exp(jax.random.uniform(jax.random.fold_in(own, position), (shards_of,), jnp.float32, least / len(pieces), high / len(pieces)))
        loudness = loudness * jnp.repeat(steps, shape[position] // shards_of).reshape([-1 if axis == position else 1 for axis in range(len(shape))])
    return loudness


def split_up(number_of, total, limit, lean):
    loads = [(1 << 20) // math.isqrt(standing ** lean) + 1 for standing in range(2, number_of + 1)]
    surplus, given = total - limit - (number_of - 1), [1] * (number_of - 1)
    while surplus > 0:
        candidates = [i for i in range(number_of - 1) if given[i] < limit]
        pool, budget = sum([loads[i] for i in candidates]), surplus
        for i in candidates:
            addition = min(limit - given[i], max(1, budget * loads[i] // pool), surplus)
            given[i] = given[i] + addition
            surplus = surplus - addition
    return np.array([limit] + given)


def ragged(key, amount, total, most, slope):
    if amount == 2:
        one = jax.random.randint(key, (), max(1, total - most), min(most, total - 1) + 1)
        return jnp.stack([one, total - one])
    sizes = jnp.asarray(split_up(amount, total, most, slope), jnp.int32)
    couples = (amount - 1) // 2
    source_of, sink = sizes[1:1 + 2 * couples:2], sizes[2:2 + 2 * couples:2]
    slack = jnp.minimum(source_of - 1, most - sink)
    shifted = jax.random.randint(jax.random.fold_in(key, 1), (couples,), 0, 1 << 20) % (slack + 1)
    sizes = sizes.at[1:1 + 2 * couples:2].set(source_of - shifted).at[2:2 + 2 * couples:2].set(sink + shifted)
    return sizes[jax.random.permutation(jax.random.fold_in(key, 2), amount)]


def normal_values(rng, dims, width, reach, cuts=(), kind=jnp.bfloat16):
    level = steps_of(rng, dims, cuts, -0.22, 0.18) if cuts else 1.0
    drawn = jax.random.normal(rng, dims, jnp.float32) * width * level
    return jnp.minimum(jnp.maximum(drawn, -reach), reach).astype(kind)


def setup_inputs(seed: int = 0) -> dict:
    splits = jax.random.split(jax.random.key(seed), 20)
    tokens = normal_values(splits[0], (TOKENS, D), 1.0, 6.0, ((0, 16),))
    cotangent = normal_values(splits[1], (TOKENS, D), 1.0, 6.0, ((0, 16),))
    lengths = ragged(splits[2], NSEQS, TOKENS, MAXLEN, 0).astype(jnp.int32)
    order = jax.random.permutation(splits[3], NSEQS).astype(jnp.int32)
    norm1_gain = jnp.clip(1.0 + 0.1 * jax.random.normal(splits[4], (D,), jnp.float32), 0.5, 1.5)
    query_weight = normal_values(splits[5], (D, HD), D ** -0.5, 0.125, ((0, 16), (1, 2)))
    key_weight = normal_values(splits[6], (D, HD), D ** -0.5, 0.125, ((0, 16), (1, 2)))
    value_weight = normal_values(splits[7], (D, HD), D ** -0.5, 0.125, ((0, 16), (1, 2)))
    beta_weight = normal_values(splits[8], (D, HEADS), D ** -0.5, 0.125, ((0, 16), (1, 2)))
    beta_bias = draw_beta_bias(jax.random.fold_in(splits[19], 71), 0)
    conv_query = normal_values(splits[10], (KERNEL, HD), 0.5, 2.5, ((1, 2),), jnp.float32)
    conv_key = normal_values(splits[11], (KERNEL, HD), 0.5, 2.5, ((1, 2),), jnp.float32)
    conv_value = normal_values(splits[12], (KERNEL, HD), 0.5, 2.5, ((1, 2),), jnp.float32)
    out_norm_gain = jnp.clip(1.0 + 0.1 * jax.random.normal(splits[13], (HEAD_DIM,), jnp.float32), 0.5, 1.5)
    out_weight = normal_values(splits[14], (HD, D), HD ** -0.5, 0.125, ((0, 2), (1, 16)))
    norm2_gain = jnp.clip(1.0 + 0.1 * jax.random.normal(splits[15], (D,), jnp.float32), 0.5, 1.5)
    gate_weight = normal_values(splits[16], (D, FF), D ** -0.5, 0.125, ((0, 16), (1, 2)))
    up_weight = normal_values(splits[17], (D, FF), D ** -0.5, 0.125, ((0, 16), (1, 2)))
    down_weight = normal_values(splits[18], (FF, D), FF ** -0.5, 0.078125, ((0, 2), (1, 16)))
    return {"tokens": tokens, "cotangent": cotangent, "lengths": lengths, "order": order, "norm1_gain": norm1_gain, "query_weight": query_weight, "key_weight": key_weight, "value_weight": value_weight, "beta_weight": beta_weight, "beta_bias": beta_bias, "conv_query": conv_query, "conv_key": conv_key, "conv_value": conv_value, "out_norm_gain": out_norm_gain, "out_weight": out_weight, "norm2_gain": norm2_gain, "gate_weight": gate_weight, "up_weight": up_weight, "down_weight": down_weight}


NORM_EPS = 1e-05
UNIT_EPS = 1e-06
HIGHEST = lax.Precision.HIGHEST

@jax.custom_vjp
def low(v):
    return lax.optimization_barrier(v.astype(jnp.bfloat16)).astype(jnp.float32)

@jax.custom_vjp
def low_back(v):
    return v

def low_keep(v):
    return (low(v), None)

def low_pass(kept, grad):
    return (grad,)

def back_keep(v):
    return (v, None)

def back_low(kept, grad):
    return (low(grad),)
low.defvjp(low_keep, low_pass)
low_back.defvjp(back_keep, back_low)

def matmul(first_op, second_op):
    return jnp.dot(first_op.astype(jnp.float32), second_op.astype(jnp.float32), precision=HIGHEST, preferred_element_type=jnp.float32)

def rms_scale(values, gain_vector):
    return values * lax.rsqrt(lax.optimization_barrier(jnp.mean(values * values, axis=-1, keepdims=True)) + NORM_EPS) * gain_vector

def unit_rows(values):
    return values * lax.rsqrt(lax.optimization_barrier(jnp.sum(values * values, axis=-1, keepdims=True)) + UNIT_EPS)

def segment_of(positions, packed):
    doc_ends = jnp.cumsum(packed).astype(jnp.int32)
    counted = lax.optimization_barrier(jnp.sum((positions[:, None] >= doc_ends[None, :]).astype(jnp.int32), axis=1)).astype(jnp.int32)
    return jnp.where(positions < 0, -1, counted).astype(jnp.int32)

def short_conv(padded, tap_weights, seg_padded, segment):
    row_count = segment.shape[0]
    summed = jnp.zeros((row_count, padded.shape[1]), jnp.float32)
    for offset in range(tap_weights.shape[0]):
        same_doc = (seg_padded[offset:offset + row_count] == segment)[:, None]
        summed = summed + jnp.where(same_doc, tap_weights[offset] * padded[offset:offset + row_count], 0.0)
    return jax.nn.silu(summed)

def delta_block(carried, queries, keys_in, values_in, strength, segment, previous):
    block_size = queries.shape[1]
    same_doc = (segment[:, None] == segment[None, :]).astype(jnp.float32)
    row_ids = lax.broadcasted_iota(jnp.int32, (block_size, block_size), 0)
    col_ids = lax.broadcasted_iota(jnp.int32, (block_size, block_size), 1)
    strict = (row_ids > col_ids).astype(jnp.float32) * same_doc
    through = (row_ids >= col_ids).astype(jnp.float32) * same_doc
    carry_in = (segment == previous).astype(jnp.float32)
    key_dots = jnp.einsum('hcd,hed->hce', keys_in, keys_in, precision=HIGHEST)
    system = jnp.eye(block_size, dtype=jnp.float32) + key_dots * strict * strength[:, None, :]
    right_side = values_in - carry_in[None, :, None] * jnp.einsum('hcd,hde->hce', keys_in, carried, precision=HIGHEST)
    fresh_values = jax.scipy.linalg.solve_triangular(system, right_side, lower=True, unit_diagonal=True)
    scores = jnp.einsum('hcd,hed->hce', queries, keys_in, precision=HIGHEST) * through * strength[:, None, :]
    outputs = carry_in[None, :, None] * jnp.einsum('hcd,hde->hce', queries, carried, precision=HIGHEST)
    outputs = outputs + jnp.einsum('hce,hef->hcf', scores, fresh_values, precision=HIGHEST)
    tail_weight = (segment == segment[-1]).astype(jnp.float32)[None, :] * strength
    updated = carry_in[-1] * carried + jnp.einsum('hcd,hce->hde', keys_in * tail_weight[:, :, None], fresh_values, precision=HIGHEST)
    return (updated, outputs)

def reference(tokens, cotangent, lengths, order, norm1_gain, query_weight, key_weight, value_weight, beta_weight, beta_bias, conv_query, conv_key, conv_value, out_norm_gain, out_weight, norm2_gain, gate_weight, up_weight, down_weight):
    blocks = TOKENS // SPAN
    packed = lengths[order].astype(jnp.int32)
    segment = segment_of(jnp.arange(TOKENS, dtype=jnp.int32), packed)
    seg_padded = segment_of(jnp.arange(TOKENS + KERNEL - 1, dtype=jnp.int32) - (KERNEL - 1), packed)
    seg_blocks = segment.reshape(blocks, SPAN)
    prev_blocks = segment_of(jnp.arange(blocks, dtype=jnp.int32) * SPAN - 1, packed)
    zero_rows = jnp.zeros((KERNEL - 1, HD), jnp.float32)

    def block_step(carried, inputs_in):
        return delta_block(carried, *inputs_in)

    def to_blocks(values):
        return values.reshape(blocks, SPAN, HEADS, HEAD_DIM).transpose(0, 2, 1, 3)

    def forward(inputs, gain_one, w_query, w_key, w_value, w_beta, bias_beta, taps_query, taps_key, taps_value, gain_out, w_out, gain_two, w_gate, w_up, w_down):
        normed = low(rms_scale(inputs, gain_one))
        proj_query = low_back(low(matmul(normed, w_query)))
        proj_key = low_back(low(matmul(normed, w_key)))
        proj_value = low_back(low(matmul(normed, w_value)))
        strength = jax.nn.sigmoid(low_back(matmul(normed, w_beta)) + bias_beta)
        conv_q = short_conv(jnp.concatenate([zero_rows, proj_query], axis=0), taps_query, seg_padded, segment)
        conv_k = short_conv(jnp.concatenate([zero_rows, proj_key], axis=0), taps_key, seg_padded, segment)
        conv_v = short_conv(jnp.concatenate([zero_rows, proj_value], axis=0), taps_value, seg_padded, segment)
        queries = low(unit_rows(conv_q.reshape(TOKENS, HEADS, HEAD_DIM)))
        keys_all = low(unit_rows(conv_k.reshape(TOKENS, HEADS, HEAD_DIM)))
        values_all = low(conv_v.reshape(TOKENS, HEADS, HEAD_DIM))
        strengths = strength.reshape(blocks, SPAN, HEADS).transpose(0, 2, 1)
        start_state = jnp.zeros((HEADS, HEAD_DIM, HEAD_DIM), jnp.float32)
        _, chain_outs = lax.scan(jax.checkpoint(block_step), start_state, (to_blocks(queries), to_blocks(keys_all), to_blocks(values_all), strengths, seg_blocks, prev_blocks))
        mixer_rows = chain_outs.transpose(0, 2, 1, 3).reshape(TOKENS, HEADS, HEAD_DIM)
        out_normed = low(rms_scale(mixer_rows, gain_out).reshape(TOKENS, HD))
        middle = inputs + low_back(matmul(out_normed, w_out))
        normed_two = low(rms_scale(middle, gain_two))
        gate_part = low_back(matmul(normed_two, w_gate))
        up_part = low_back(matmul(normed_two, w_up))
        hidden = low(jax.nn.silu(gate_part) * up_part)
        return middle + matmul(hidden, w_down)
    arrays = (tokens.astype(jnp.float32), norm1_gain, query_weight.astype(jnp.float32), key_weight.astype(jnp.float32), value_weight.astype(jnp.float32), beta_weight.astype(jnp.float32), beta_bias, conv_query, conv_key, conv_value, out_norm_gain, out_weight.astype(jnp.float32), norm2_gain, gate_weight.astype(jnp.float32), up_weight.astype(jnp.float32), down_weight.astype(jnp.float32))
    result, pullback = jax.vjp(forward, *arrays)
    gradients = pullback(cotangent.astype(jnp.float32))
    return (result.astype(jnp.bfloat16), gradients[0], gradients[1], gradients[2], gradients[3], gradients[4], gradients[5], gradients[6], gradients[7], gradients[8], gradients[9], gradients[10], gradients[11], gradients[12], gradients[13], gradients[14], gradients[15])
```

```python
import jax
import jax.numpy as jnp
from jax import lax
from jax.experimental import pallas as pl
from jax.experimental.pallas import tpu as pltpu
from jax.sharding import Mesh
from jax.sharding import PartitionSpec as P

HEAD_DIM = 128
CHUNK = 128
SUB = 2
NORM_EPS = 1e-05
UNIT_EPS = 1e-06
F32 = jnp.float32
BF16 = jnp.bfloat16


def mm(a, b):
    return jnp.dot(a, b, preferred_element_type=F32)


def mm_nt(a, b):
    return lax.dot_general(a, b, (((1,), (1,)), ((), ())), preferred_element_type=F32)


def mm_tn(a, b):
    return lax.dot_general(a, b, (((0,), (0,)), ((), ())), preferred_element_type=F32)


def split(a):
    high = a.astype(BF16)
    return high, (a - high.astype(F32)).astype(BF16)


def mm3(a, b):
    (ah, al), (bh, bl) = a, b
    return mm(ah, bh) + (mm(ah, bl) + mm(al, bh))


def iotas():
    rows = lax.broadcasted_iota(jnp.int32, (CHUNK, CHUNK), 0)
    cols = lax.broadcasted_iota(jnp.int32, (CHUNK, CHUNK), 1)
    return rows, cols


def inverses(systems):
    rows, cols = iotas()
    eye = (rows == cols).astype(F32)
    same8 = (rows >> 3) == (cols >> 3)
    low = [jnp.where(same8, a, 0.0) for a in systems]
    low_s = [split(n) for n in low]
    sq = [mm3(n, n) for n in low_s]
    sq_s = [split(n) for n in sq]
    first = [eye - n for n in low]
    quad = [mm3(n, n) for n in sq_s]
    t = [f + mm3(split(f), s) for f, s in zip(first, sq_s)]
    t = [x + mm3(split(x), split(n)) for x, n in zip(t, quad)]
    for level in (3, 4, 5, 6):
        joined = ((rows >> (level + 1)) == (cols >> (level + 1))) & ((rows >> level) != (cols >> level))
        off = [split(jnp.where(joined, a, 0.0)) for a in systems]
        t_s = [split(x) for x in t]
        mid = [split(mm3(o, x)) for o, x in zip(off, t_s)]
        t = [x - mm3(xs, m) for x, xs, m in zip(t, t_s, mid)]
    return t


def silu_parts(pre):
    sig = jax.nn.sigmoid(pre)
    return pre * sig, sig


def forward_one(q_ref, proj_ref, halo_ref, taps_ref, bias_ref, col_ref, row_ref,
                pre_ref, qkv_ref, beta_ref, t_ref, x_ref, last_ref, ext, state):
    step = pl.program_id(0)
    heads = state.shape[0]
    width = heads * HEAD_DIM
    rows = SUB * CHUNK
    rid, cid = iotas()

    @pl.when(step == 0)
    def _():
        ext[0:8, :] = halo_ref[:, : 3 * width].astype(F32)
        eye = (rid == cid).astype(F32)
        for h in range(heads):
            state[h, :, :CHUNK] = eye
            state[h, :, CHUNK:] = jnp.zeros((CHUNK, CHUNK), F32)

    raw = proj_ref[...]
    ext[8 : 8 + rows, :] = raw[:, : 3 * width].astype(F32)
    beta = jax.nn.sigmoid(raw[:, 3 * width :].astype(F32) + bias_ref[...])
    beta_ref[...] = beta
    col = col_ref[...]
    pre = taps_ref[3:4, :] * ext[8 : 8 + rows, :]
    for k in (1, 2, 3):
        pre = pre + taps_ref[3 - k : 4 - k, :] * (col[:, 2 + k : 3 + k] * ext[8 - k : 8 - k + rows, :])
    pre_ref[...] = pre
    tail = ext[rows : rows + 8, :]
    ext[0:8, :] = tail
    conv, _ = silu_parts(pre)
    parts = []
    for i in range(3 * heads):
        part = conv[:, i * HEAD_DIM : (i + 1) * HEAD_DIM]
        if i < 2 * heads:
            part = part * lax.rsqrt(jnp.sum(part * part, axis=1, keepdims=True) + UNIT_EPS)
        parts.append(part.astype(BF16))
        qkv_ref[:, i * HEAD_DIM : (i + 1) * HEAD_DIM] = parts[-1]

    pairs, systems = [], []
    for s in range(SUB):
        at = slice(s * CHUNK, (s + 1) * CHUNK)
        seg_row = row_ref[0:1, at]
        strict = (col[at, 0:1] == seg_row) & (rid > cid)
        beta_t = beta[at, :].T
        carry = col[at, 1:2]
        for h in range(heads):
            k = parts[heads + h][at, :]
            v = parts[2 * heads + h][at, :]
            systems.append(jnp.where(strict, mm_nt(k, k), 0.0) * beta_t[h : h + 1, :])
            kf = k.astype(F32)
            ck = (carry * kf).astype(BF16)
            kt = (col[at, 2:3] * beta[at, h : h + 1] * kf).astype(BF16)
            pairs.append((s, h, v, ck, kt, carry[CHUNK - 1 : CHUNK, :]))
    ts = inverses(systems)
    maps = []
    for (s, h, v, ck, kt, last), t in zip(pairs, ts):
        tb = t.astype(BF16)
        t_ref[h, s] = tb
        uw = mm(tb, jnp.concatenate([v, ck], axis=1)).astype(BF16)
        maps.append(mm_tn(kt, uw))
    for (s, h, v, ck, kt, last), bp in zip(pairs, maps):
        x = state[h]
        xb = x.astype(BF16)
        x_ref[h, s] = xb
        new = last * x - mm(bp[:, CHUNK:].astype(BF16), xb)
        state[h, :, :CHUNK] = new[:, :CHUNK]
        state[h, :, CHUNK:] = new[:, CHUNK:] + bp[:, :CHUNK]

    @pl.when(step == pl.num_programs(0) - 1)
    def _():
        last_ref[...] = state[...]


def forward_two(q_ref, qkv_ref, beta_ref, t_ref, x_ref, start_ref, gain_ref, col_ref, row_ref,
                low_ref, mixed_ref, s_ref, u_ref):
    heads = t_ref.shape[0]
    rid, cid = iotas()
    col = col_ref[...]
    for s in range(SUB):
        at = slice(s * CHUNK, (s + 1) * CHUNK)
        seg_row = row_ref[0:1, at]
        through = (col[at, 0:1] == seg_row) & (rid >= cid)
        beta_t = beta_ref[at, :].T
        carry = col[at, 1:2]
        for h in range(heads):
            q = qkv_ref[at, h * HEAD_DIM : (h + 1) * HEAD_DIM]
            k = qkv_ref[at, (heads + h) * HEAD_DIM : (heads + h + 1) * HEAD_DIM]
            v = qkv_ref[at, (2 * heads + h) * HEAD_DIM : (2 * heads + h + 1) * HEAD_DIM]
            x = x_ref[h, s]
            state = (mm(x[:, :CHUNK], start_ref[h].astype(BF16)) + x[:, CHUNK:].astype(F32)).astype(BF16)
            s_ref[h, s] = state
            kq = mm(jnp.concatenate([k, q], axis=0), state)
            right = (v.astype(F32) - carry * kq[:CHUNK]).astype(BF16)
            u = mm(t_ref[h, s], right).astype(BF16)
            u_ref[h, s] = u
            scores = (jnp.where(through, mm_nt(q, k), 0.0) * beta_t[h : h + 1, :]).astype(BF16)
            mixed = carry * kq[CHUNK:] + mm(scores, u)
            mixed_ref[at, h * HEAD_DIM : (h + 1) * HEAD_DIM] = mixed
            scale = lax.rsqrt(jnp.mean(mixed * mixed, axis=1, keepdims=True) + NORM_EPS)
            low_ref[at, h * HEAD_DIM : (h + 1) * HEAD_DIM] = (mixed * scale * gain_ref[...]).astype(BF16)


def backward_one(q_ref, dout_ref, mixed_ref, gain_ref, qkv_ref, beta_ref, t_ref, col_ref, row_ref,
                 do_ref, z_ref, vt_ref, y_ref, last_ref, dgain_ref, state):
    step = pl.program_id(0)
    heads = state.shape[0]
    rid, cid = iotas()

    @pl.when(step == 0)
    def _():
        eye = (rid == cid).astype(F32)
        for h in range(heads):
            state[h, :, :CHUNK] = eye
            state[h, :, CHUNK:] = jnp.zeros((CHUNK, CHUNK), F32)
        dgain_ref[...] = jnp.zeros_like(dgain_ref)

    col = col_ref[...]
    gain = gain_ref[...]
    pairs = []
    dgain = jnp.zeros((1, HEAD_DIM), F32)
    for s in reversed(range(SUB)):
        at = slice(s * CHUNK, (s + 1) * CHUNK)
        seg_row = row_ref[0:1, at]
        through_t = (col[at, 0:1] == seg_row) & (cid >= rid)
        carry = col[at, 1:2]
        for h in range(heads):
            q = qkv_ref[at, h * HEAD_DIM : (h + 1) * HEAD_DIM]
            k = qkv_ref[at, (heads + h) * HEAD_DIM : (heads + h + 1) * HEAD_DIM]
            mixed = mixed_ref[at, h * HEAD_DIM : (h + 1) * HEAD_DIM]
            dy = dout_ref[at, h * HEAD_DIM : (h + 1) * HEAD_DIM].astype(F32)
            scale = lax.rsqrt(jnp.mean(mixed * mixed, axis=1, keepdims=True) + NORM_EPS)
            normed = mixed * scale
            dgain = dgain + jnp.sum(dy * normed, axis=0, keepdims=True)
            gdy = gain * dy
            do = (scale * (gdy - normed * jnp.mean(normed * gdy, axis=1, keepdims=True))).astype(BF16)
            do_ref[at, h * HEAD_DIM : (h + 1) * HEAD_DIM] = do
            beta = beta_ref[at, h : h + 1]
            scores_t = (jnp.where(through_t, mm_nt(k, q), 0.0) * beta).astype(BF16)
            kf = k.astype(F32)
            kt = (col[at, 2:3] * beta * kf).astype(BF16)
            ck = (carry * kf).astype(BF16)
            cq = (carry * q.astype(F32)).astype(BF16)
            md = mm(scores_t, do).astype(BF16)
            zv = mm_tn(t_ref[h, s], jnp.concatenate([md, kt], axis=1))
            z_ref[h, s] = zv[:, :CHUNK]
            zvb = zv.astype(BF16)
            vt_ref[h, s] = zvb[:, CHUNK:]
            dp = mm_tn(ck, zvb)
            d = mm_tn(cq, do) - dp[:, :CHUNK]
            pairs.append((s, h, d, dp[:, CHUNK:].astype(BF16), carry[CHUNK - 1 : CHUNK, :]))
    dgain_ref[...] += dgain
    for s, h, d, p, last in pairs:
        y = state[h]
        yb = y.astype(BF16)
        y_ref[h, s] = yb
        new = last * y - mm(p, yb)
        state[h, :, :CHUNK] = new[:, :CHUNK]
        state[h, :, CHUNK:] = new[:, CHUNK:] + d

    @pl.when(step == pl.num_programs(0) - 1)
    def _():
        last_ref[...] = state[...]


def backward_two(q_ref, pre_ref, proj_ref, taps_ref, qkv_ref, beta_ref, do_ref, z_ref, vt_ref, y_ref, s_ref, u_ref,
                 end_ref, col_ref, row_ref,
                 dproj_ref, head_ref, dtaps_ref, dbias_ref, ext):
    step = pl.program_id(0)
    heads = z_ref.shape[0]
    width = heads * HEAD_DIM
    rows = SUB * CHUNK
    rid, cid = iotas()

    @pl.when(step == 0)
    def _():
        ext[rows : rows + 8, :] = jnp.zeros((8, 3 * width), F32)
        dtaps_ref[...] = jnp.zeros_like(dtaps_ref)
        dbias_ref[...] = jnp.zeros_like(dbias_ref)

    col = col_ref[...]
    lane = lax.broadcasted_iota(jnp.int32, (CHUNK, 128), 1)
    dbias = jnp.zeros((1, 128), F32)
    for s in range(SUB):
        at = slice(s * CHUNK, (s + 1) * CHUNK)
        seg_row = row_ref[0:1, at]
        same = col[at, 0:1] == seg_row
        through_t = same & (cid >= rid)
        strict_t = same & (cid > rid)
        carry = col[at, 1:2]
        tail = col[at, 2:3]
        dlog = jnp.zeros((CHUNK, 128), F32)
        for h in range(heads):
            q = qkv_ref[at, h * HEAD_DIM : (h + 1) * HEAD_DIM]
            k = qkv_ref[at, (heads + h) * HEAD_DIM : (heads + h + 1) * HEAD_DIM]
            do = do_ref[at, h * HEAD_DIM : (h + 1) * HEAD_DIM]
            beta = beta_ref[at, h : h + 1]
            state = s_ref[h, s]
            u = u_ref[h, s]
            y = y_ref[h, s]
            g = (mm(y[:, :CHUNK], end_ref[h].astype(BF16)) + y[:, CHUNK:].astype(F32)).astype(BF16)
            dr = z_ref[h, s] + mm(vt_ref[h, s], g)
            drb = dr.astype(BF16)
            kk = mm_nt(k, k)
            kq = mm_nt(k, q)
            dm_t = jnp.where(through_t, mm_nt(u, do), 0.0)
            da_t = jnp.where(strict_t, -mm_nt(u, drb), 0.0)
            ug = mm_nt(u, g)
            kf = k.astype(F32)
            dbeta = jnp.sum(dm_t * kq + da_t * kk + tail * (kf * ug), axis=1, keepdims=True)
            dqk_t = (dm_t * beta).astype(BF16)
            dkk_t = da_t * beta
            dkk = (dkk_t + dkk_t.T).astype(BF16)
            sd = mm_nt(jnp.concatenate([do, drb], axis=0), state)
            dq = carry * sd[:CHUNK] + mm_tn(dqk_t, k)
            dk = mm(dqk_t, q) + mm(dkk, k) + (tail * beta) * ug - carry * sd[CHUNK:]
            dl = dbeta * beta * (1.0 - beta)
            dlog = jnp.where(lane == h, dl, dlog)
            qf = q.astype(F32)
            for i, d, unit in ((h, dq, qf), (heads + h, dk, kf), (2 * heads + h, dr, None)):
                lanes = slice(i * HEAD_DIM, (i + 1) * HEAD_DIM)
                pre = pre_ref[at, lanes]
                conv, sig = silu_parts(pre)
                if unit is not None:
                    scale = lax.rsqrt(jnp.sum(conv * conv, axis=1, keepdims=True) + UNIT_EPS)
                    d = (d - unit * jnp.sum(unit * d, axis=1, keepdims=True)) * scale
                ext[at, lanes] = d * (sig * (1.0 + pre * (1.0 - sig)))
        dproj_ref[at, 3 * width :] = dlog.astype(BF16)
        dbias = dbias + jnp.sum(dlog, axis=0, keepdims=True)
    dbias_ref[...] += dbias
    proj = proj_ref[:, : 3 * width].astype(F32)
    total = taps_ref[3:4, :] * ext[0:rows, :]
    dtaps_ref[3:4, :] += jnp.sum(proj * ext[0:rows, :], axis=0, keepdims=True)
    for k in (1, 2, 3):
        moved = col[:, 5 + k : 6 + k] * ext[k : k + rows, :]
        total = total + taps_ref[3 - k : 4 - k, :] * moved
        dtaps_ref[3 - k : 4 - k, :] += jnp.sum(proj * moved, axis=0, keepdims=True)
    dproj_ref[:, : 3 * width] = total.astype(BF16)
    first = ext[0:8, :]
    ext[rows : rows + 8, :] = first

    @pl.when(step == pl.num_programs(0) - 1)
    def _():
        head_ref[...] = first


def call(body, q, ins, outs, scratch, rows, chip_rows, reverse, flops, name):
    steps = rows // (SUB * CHUNK)
    per_chip = chip_rows // (SUB * CHUNK)

    def at(i):
        return steps - 1 - i if reverse else i

    def spec(shape, kind):
        if kind == "seq":
            return pl.BlockSpec((SUB * CHUNK, shape[1]), lambda i, qr: (at(i), 0))
        if kind == "rel":
            return pl.BlockSpec(
                (SUB * CHUNK, shape[1]),
                lambda i, qr: (((at(i) // per_chip) ^ qr[0]) * per_chip + at(i) % per_chip, 0),
            )
        if kind == "lane":
            return pl.BlockSpec((shape[0], SUB * CHUNK), lambda i, qr: (0, at(i)))
        if kind == "blk":
            return pl.BlockSpec((shape[0], SUB) + shape[2:], lambda i, qr: (0, at(i), 0, 0))
        return pl.BlockSpec(shape, lambda i, qr: (0,) * len(shape))

    nbytes = sum(a.size * a.dtype.itemsize for a, _ in ins) + sum(a.size * a.dtype.itemsize for a, _ in outs)
    return pl.pallas_call(
        body,
        grid_spec=pltpu.PrefetchScalarGridSpec(
            num_scalar_prefetch=1,
            grid=(steps,),
            in_specs=[spec(a.shape, kind) for a, kind in ins],
            out_specs=[spec(a.shape, kind) for a, kind in outs],
            scratch_shapes=scratch,
        ),
        out_shape=[a for a, _ in outs],
        compiler_params=pltpu.CompilerParams(
            dimension_semantics=("arbitrary",), vmem_limit_bytes=48 * 1024 * 1024
        ),
        cost_estimate=pl.CostEstimate(flops=flops, bytes_accessed=nbytes, transcendentals=0),
        name=name,
    )(q, *[a for a, _ in ins])


def shape(dims, dtype):
    return jax.ShapeDtypeStruct(dims, dtype)


def mixer_forward_one(q, proj, halo, taps, bias, cols, lanes, chip_rows):
    rows = proj.shape[0]
    width = taps.shape[1]
    heads = width // (3 * HEAD_DIM)
    n = rows // CHUNK
    return call(
        forward_one, q,
        [(proj, "rel"), (halo, "all"), (taps, "all"), (bias, "all"), (cols, "seq"), (lanes, "lane")],
        [(shape((rows, width), F32), "seq"), (shape((rows, width), BF16), "seq"), (shape((rows, 128), F32), "seq"),
         (shape((heads, n, CHUNK, CHUNK), BF16), "blk"), (shape((heads, n, CHUNK, 2 * CHUNK), BF16), "blk"),
         (shape((heads, CHUNK, 2 * CHUNK), F32), "all")],
        [pltpu.VMEM((SUB * CHUNK + 8, width), F32), pltpu.VMEM((heads, CHUNK, 2 * CHUNK), F32)],
        rows, chip_rows, False, 2 * heads * n * 50 * CHUNK**3, "delta_forward_one")


def mixer_forward_two(q, qkv, beta, t, x, start, gain, cols, lanes, chip_rows):
    rows = qkv.shape[0]
    heads, n = t.shape[:2]
    return call(
        forward_two, q,
        [(qkv, "seq"), (beta, "seq"), (t, "blk"), (x, "blk"), (start, "all"), (gain, "all"), (cols, "seq"), (lanes, "lane")],
        [(shape((rows, heads * HEAD_DIM), BF16), "rel"), (shape((rows, heads * HEAD_DIM), F32), "seq"),
         (shape((heads, n, CHUNK, CHUNK), BF16), "blk"), (shape((heads, n, CHUNK, CHUNK), BF16), "blk")],
        [], rows, chip_rows, False, 2 * heads * n * 8 * CHUNK**3, "delta_forward_two")


def mixer_backward_one(q, dout, mixed, gain, qkv, beta, t, cols, lanes, chip_rows):
    rows = qkv.shape[0]
    heads, n = t.shape[:2]
    return call(
        backward_one, q,
        [(dout, "rel"), (mixed, "seq"), (gain, "all"), (qkv, "seq"), (beta, "seq"), (t, "blk"), (cols, "seq"), (lanes, "lane")],
        [(shape((rows, heads * HEAD_DIM), BF16), "seq"), (shape((heads, n, CHUNK, CHUNK), F32), "blk"),
         (shape((heads, n, CHUNK, CHUNK), BF16), "blk"), (shape((heads, n, CHUNK, 2 * CHUNK), BF16), "blk"),
         (shape((heads, CHUNK, 2 * CHUNK), F32), "all"), (shape((1, HEAD_DIM), F32), "all")],
        [pltpu.VMEM((heads, CHUNK, 2 * CHUNK), F32)],
        rows, chip_rows, True, 2 * heads * n * 12 * CHUNK**3, "delta_backward_one")


def mixer_backward_two(q, pre, proj, taps, qkv, beta, do, z, vt, y, s, u, end, cols, lanes, chip_rows):
    rows, width = pre.shape
    heads, n = z.shape[:2]
    return call(
        backward_two, q,
        [(pre, "seq"), (proj, "rel"), (taps, "all"), (qkv, "seq"), (beta, "seq"), (do, "seq"), (z, "blk"), (vt, "blk"),
         (y, "blk"), (s, "blk"), (u, "blk"), (end, "all"), (cols, "seq"), (lanes, "lane")],
        [(shape((rows, width + 128), BF16), "rel"), (shape((8, width), F32), "all"), (shape((4, width), F32), "all"),
         (shape((1, 128), F32), "all")],
        [pltpu.VMEM((SUB * CHUNK + 8, width), F32)],
        rows, chip_rows, True, 2 * heads * n * 14 * CHUNK**3, "delta_backward_two")


PLANE = 4
SWAP = [(0, 1), (1, 0)]
DIAGONAL = [(0, 3), (1, 2), (2, 1), (3, 0)]
PAD = 128


def send(block, axis):
    return lax.ppermute(block, axis, DIAGONAL if axis == ("y", "x") else SWAP)


def along(block, step):
    n = lax.axis_size("z")
    return lax.ppermute(block, "z", [(i, i + step) for i in range(n) if 0 <= i + step < n])


def gather_rows(block):
    half = block.shape[0] // 2
    from_x = send(block, "x")
    from_y = send(block, "y")
    far_top = send(from_y[:half], "x")
    far_low = send(from_x[half:], "y")
    return [block, from_x, from_y, far_top, far_low]


def widen(pieces, head):
    rows = []
    for piece in pieces:
        other = send(piece, "head")
        rows.append(
            jnp.where(head == 0, jnp.concatenate([piece, other], 1), jnp.concatenate([other, piece], 1))
        )
    return jnp.concatenate(rows, 0)


def scatter_rows(part):
    size = part.shape[0] // PLANE
    half = size // 2
    own, at_x, at_y, far = (part[i * size : (i + 1) * size] for i in range(PLANE))
    top = send(far[:half], "x")
    low = send(far[half:], "y")
    at_y = jnp.concatenate([(at_y[:half].astype(F32) + top.astype(F32)).astype(BF16), at_y[half:]], 0)
    at_x = jnp.concatenate([at_x[:half], (at_x[half:].astype(F32) + low.astype(F32)).astype(BF16)], 0)
    from_x = send(at_x, "x")
    from_y = send(at_y, "y")
    return own.astype(F32) + from_x.astype(F32) + from_y.astype(F32)


def half_of(array, head, axis):
    size = array.shape[axis] // 2
    return lax.dynamic_slice_in_dim(array, head * size, size, axis)


def reduce_cores(left, right_rows, head):
    other = mm_nt(left, half_of(right_rows, 1 - head, 0)).astype(BF16)
    own = mm_nt(left, half_of(right_rows, head, 0))
    return (own + send(other, "head").astype(F32)).astype(BF16)


def in_order(pieces, place):
    result = []
    for i in range(PLANE):
        out = pieces[i]
        for j in range(PLANE):
            if j != i:
                out = jnp.where(place == (i ^ j), pieces[j], out)
        result.append(out)
    return result


def exchange(pieces):
    return [pieces[0], send(pieces[1], "x"), send(pieces[2], "y"), send(pieces[3], ("y", "x"))]


def row_sum(values):
    own = jnp.sum(values, axis=1)
    return (own + send(own, "head"))[:, None]


def everywhere(values):
    for axis in ("x", "y"):
        values = values + send(values, axis)
    n = lax.axis_size("z")
    step = 1
    while step < n:
        values = values + lax.ppermute(values, "z", [(i, i ^ step) for i in range(n)])
        step *= 2
    return values


def segment_of(positions, doc_ends):
    counted = jnp.sum((positions[..., None] >= doc_ends).astype(jnp.int32), axis=-1)
    return jnp.where(positions < 0, -1, counted)


def mask_arrays(first, rows, doc_ends):
    def seg_at(offset):
        return segment_of(first + offset + jnp.arange(rows, dtype=jnp.int32), doc_ends)

    places = jnp.arange(rows, dtype=jnp.int32)
    starts = (places // CHUNK) * CHUNK
    own = seg_at(0)
    before = segment_of(first + starts - 1, doc_ends)
    last = segment_of(first + starts + CHUNK - 1, doc_ends)
    columns = [own, own == before, own == last]
    columns += [seg_at(-k) == own for k in (1, 2, 3)] + [seg_at(k) == own for k in (1, 2, 3)]
    columns = jnp.stack([c.astype(F32) for c in columns] + [jnp.zeros((rows,), F32)] * 7, axis=1)
    lanes = jnp.concatenate([own.astype(F32)[None], jnp.zeros((7, rows), F32)], 0)
    return columns, lanes


def ff_starts(total, place):
    tiles = total // 128
    base, extra = tiles // PLANE, tiles % PLANE
    most = base + (1 if extra else 0)
    start = (place * base + jnp.minimum(place, extra)) * 128
    own = (base + (place < extra).astype(jnp.int32)) * 128
    sizes = [(base + (1 if i < extra else 0)) * 128 for i in range(PLANE)]
    return start, own, most * 128, sizes


def body(
    tokens,
    cotangent,
    lengths,
    order,
    norm1_gain,
    query_weight,
    key_weight,
    value_weight,
    beta_weight,
    beta_bias,
    conv_query,
    conv_key,
    conv_value,
    out_norm_gain,
    out_weight,
    norm2_gain,
    gate_weight,
    up_weight,
    down_weight,
):
    chip_rows, model = tokens.shape
    depth = query_weight.shape[0]
    units = gate_weight.shape[1]
    rows = PLANE * chip_rows
    half = model // 2
    heads = beta_weight.shape[1] // PLANE
    width = heads * HEAD_DIM
    head = lax.axis_index("head")
    z = lax.axis_index("z")
    place = 2 * lax.axis_index("y") + lax.axis_index("x")
    place_array = jnp.reshape(place, (1,)).astype(jnp.int32)

    doc_ids = jnp.arange(lengths.shape[0], dtype=jnp.int32)
    packed = jnp.sum(jnp.where(order[:, None] == doc_ids[None, :], lengths[None, :], 0), axis=1)
    doc_ends = jnp.cumsum(packed)
    columns, lanes = mask_arrays(z * rows, rows, doc_ends)

    def mixer_piece(j):
        to = place ^ j
        parts = [
            lax.dynamic_slice_in_dim(w, to * width, width, 1) for w in (query_weight, key_weight, value_weight)
        ]
        beta = lax.dynamic_slice_in_dim(beta_weight, to * heads, heads, 1)
        return jnp.concatenate(parts + [jnp.pad(beta, ((0, 0), (0, 128 - heads)))], 1)

    def gather_weight(pieces):
        return lax.all_gather(jnp.concatenate(in_order(exchange(pieces), place), 0), "z", axis=0, tiled=True)

    w_mix = gather_weight([mixer_piece(j) for j in range(PLANE)])
    inputs = tokens.astype(F32)
    scale_one = lax.rsqrt(jnp.mean(inputs * inputs, axis=1, keepdims=True) + NORM_EPS)
    normed_half = half_of((inputs * scale_one * norm1_gain).astype(BF16), head, 1)
    x_one = widen(gather_rows(normed_half), head)
    out_rows = out_weight.T
    w_out = gather_weight(
        [lax.dynamic_slice_in_dim(out_rows, (place ^ j) * width, width, 1) for j in range(PLANE)]
    )
    ff_sizes = ff_starts(units, place)[3]

    def ff_piece(weights, j):
        start, own, most, _ = ff_starts(units, place ^ j)
        parts = []
        for w in weights:
            cut = lax.dynamic_slice_in_dim(jnp.pad(w, ((0, 0), (0, PAD))), start, most, 1)
            parts.append(jnp.where(lax.broadcasted_iota(jnp.int32, cut.shape, 1) < own, cut, 0))
        return jnp.concatenate(parts, 1)

    w_gu = gather_weight([ff_piece((gate_weight, up_weight), j) for j in range(PLANE)])
    down_rows = down_weight.T
    w_down = gather_weight([ff_piece((down_rows,), j) for j in range(PLANE)])
    dy = widen(gather_rows(half_of(cotangent, head, 1)), head)

    proj = mm(x_one, w_mix).astype(BF16)
    place_last = (PLANE - 1) ^ place
    tail_rows = lax.dynamic_slice_in_dim(proj, (place_last + 1) * chip_rows - 8, 8, 0)
    halo = along(tail_rows, 1)
    my_columns = [lax.dynamic_slice_in_dim(t, place * width, width, 1) for t in (conv_query, conv_key, conv_value)]
    taps = jnp.concatenate(my_columns, 1)
    bias = jnp.pad(lax.dynamic_slice_in_dim(beta_bias, place * heads, heads, 0), (0, 128 - heads))[None]
    gain_out = out_norm_gain[None]
    pre, qkv, beta, t, prefix, last = mixer_forward_one(
        place_array, proj, halo, taps, bias, columns, lanes, chip_rows
    )

    def chain(maps, step):
        start = jnp.zeros((heads, HEAD_DIM, HEAD_DIM), F32)
        for _ in range(lax.axis_size("z") - 1):
            moved = jnp.einsum("hij,hjk->hik", maps[:, :, :HEAD_DIM], start, precision=lax.Precision.HIGHEST)
            start = along(moved + maps[:, :, HEAD_DIM:], step)
        return start

    state_in = chain(last, 1)
    out_low, mixed, states, fresh = mixer_forward_two(
        place_array, qkv, beta, t, prefix, state_in, gain_out, columns, lanes, chip_rows
    )
    middle = half_of(inputs, head, 1) + scatter_rows(reduce_cores(out_low, w_out, head))

    gain_two = half_of(norm2_gain, head, 0)
    scale_two = lax.rsqrt(row_sum(middle * middle) / model + NORM_EPS)
    x_two = widen(gather_rows((middle * scale_two * gain_two).astype(BF16)), head)
    wide = w_down.shape[1]
    gate_up = mm(x_two, w_gu)
    gate, up = gate_up[:, :wide], gate_up[:, wide:]
    dhidden = mm(dy, w_down)
    sig = jax.nn.sigmoid(gate)
    hidden = (gate * sig * up).astype(BF16)
    dgate = (dhidden * up * sig * (1.0 + gate * (1.0 - sig))).astype(BF16)
    dup = (dhidden * gate * sig).astype(BF16)
    dgu = jnp.concatenate([dgate, dup], 1)
    dnormed_two = scatter_rows(reduce_cores(dgu, w_gu, head))

    def scatter_weight(grad):
        return lax.psum_scatter(grad.astype(BF16), "z", scatter_dimension=0, tiled=True)

    def return_weight(grad):
        pieces = [lax.dynamic_slice_in_dim(grad, (place ^ j) * depth, depth, 0) for j in range(PLANE)]
        return in_order(exchange(pieces), place)

    grad_gu = scatter_weight(mm_tn(x_two, dgu))
    grad_down = scatter_weight(mm_tn(dy, hidden))
    ffn_out = scatter_rows(reduce_cores(hidden, w_down, head))
    output_half = (middle + ffn_out).astype(BF16)

    normed_mid = middle * scale_two
    gdy = dnormed_two * gain_two
    dmiddle = half_of(cotangent, head, 1).astype(F32) + scale_two * (
        gdy - normed_mid * (row_sum(normed_mid * gdy) / model)
    )
    grad_norm2 = jnp.sum(dnormed_two * normed_mid, axis=0)
    dmix = widen(gather_rows(dmiddle.astype(BF16)), head)

    dout = mm(dmix, w_out)
    grad_out = scatter_weight(mm_tn(dmix, out_low))
    do, zed, vt, suffix, first, grad_onorm = mixer_backward_one(
        place_array, dout, mixed, gain_out, qkv, beta, t, columns, lanes, chip_rows
    )
    state_end = chain(first, -1)
    dproj, da_head, grad_taps, grad_bias = mixer_backward_two(
        place_array, pre, proj, taps, qkv, beta, do, zed, vt, suffix, states, fresh, state_end, columns, lanes, chip_rows
    )
    da_next = along(da_head, -1)
    tail_at = (place_last + 1) * chip_rows - 8
    tail_proj = lax.dynamic_slice_in_dim(proj, tail_at, 8, 0)[:, : 3 * width].astype(F32)
    places = z * rows + rows - 8 + jnp.arange(8, dtype=jnp.int32)
    own_seg = segment_of(places, doc_ends)
    extra = jnp.zeros((8, 3 * width), F32)
    extra_taps = [jnp.zeros((3 * width,), F32)]
    for k in (1, 2, 3):
        same = (segment_of(places + k, doc_ends) == own_seg) & (jnp.arange(8) + k >= 8)
        moved = jnp.where(same[:, None], jnp.concatenate([jnp.zeros((8 - k, 3 * width), F32), da_next[:k]], 0), 0.0)
        extra = extra + taps[3 - k] * moved
        extra_taps.insert(0, jnp.sum(tail_proj * moved, axis=0))
    grad_taps = grad_taps + jnp.stack(extra_taps)
    tail_old = lax.dynamic_slice_in_dim(dproj, tail_at, 8, 0)
    tail_new = (tail_old.astype(F32) + jnp.pad(extra, ((0, 0), (0, 128)))).astype(BF16)
    dproj = lax.dynamic_update_slice_in_dim(dproj, tail_new, tail_at, 0)

    grad_mix = scatter_weight(mm_tn(x_one, dproj))
    dnormed_one = scatter_rows(reduce_cores(dproj, w_mix, head))
    inputs_half = half_of(inputs, head, 1)
    normed_in = inputs_half * scale_one
    gdy = dnormed_one * half_of(norm1_gain, head, 0)
    input_half = dmiddle + scale_one * (gdy - normed_in * (row_sum(normed_in * gdy) / model))
    grad_norm1 = jnp.sum(dnormed_one * normed_in, axis=0)

    small_taps = jnp.zeros((PLANE, 4, 3 * width), F32)
    small_taps = lax.dynamic_update_slice(small_taps, grad_taps[None], (place, 0, 0))
    small_bias = jnp.zeros((PLANE, 128), F32)
    small_bias = lax.dynamic_update_slice(small_bias, grad_bias, (place, 0))
    flat = jnp.concatenate(
        [
            small_taps.reshape(-1, 128),
            small_bias,
            grad_onorm,
            jnp.zeros((3, 128), F32),
            grad_norm1.reshape(-1, 128),
            grad_norm2.reshape(-1, 128),
        ],
        0,
    )
    flat = everywhere(flat)
    cut = PLANE * 12 * width // 128
    taps_sum = flat[:cut].reshape(PLANE, 4, 3, width)
    taps_sum = taps_sum.transpose(2, 1, 0, 3).reshape(3, 4, PLANE * width)
    bias_sum = flat[cut : cut + PLANE, :heads].reshape(-1)
    shared = flat[cut + PLANE :]
    shared_other = send(shared, "head")
    onorm_sum = shared[0] + shared_other[0]
    per = half // 128

    def both(own, other):
        own, other = own.reshape(-1), other.reshape(-1)
        return jnp.where(head == 0, jnp.concatenate([own, other]), jnp.concatenate([other, own]))

    norm1_sum = both(shared[4 : 4 + per], shared_other[4 : 4 + per])
    norm2_sum = both(shared[4 + per :], shared_other[4 + per :])

    mix_home = return_weight(grad_mix)
    out_home = return_weight(grad_out)
    gu_home = return_weight(grad_gu)
    down_home = return_weight(grad_down)

    def columns_of(home, start, sizes):
        return jnp.concatenate([p[:, start : start + s] for p, s in zip(home, sizes)], 1).astype(F32)

    even = [width] * PLANE
    output = widen([output_half], head)
    input_grad = widen([input_half], head)
    return (
        output,
        input_grad,
        norm1_sum,
        columns_of(mix_home, 0, even),
        columns_of(mix_home, width, even),
        columns_of(mix_home, 2 * width, even),
        columns_of(mix_home, 3 * width, [heads] * PLANE),
        bias_sum,
        taps_sum[0],
        taps_sum[1],
        taps_sum[2],
        onorm_sum,
        columns_of(out_home, 0, even).T,
        norm2_sum,
        columns_of(gu_home, 0, ff_sizes),
        columns_of(gu_home, wide, ff_sizes),
        columns_of(down_home, 0, ff_sizes).T,
    )


def solution(mesh):
    planes = mesh.shape["seq"] // PLANE
    grid = Mesh(mesh.devices.reshape(planes, 2, 2, 2), ("z", "y", "x", "head"))
    seq = ("z", "y", "x")
    return jax.shard_map(
        body,
        mesh=grid,
        in_specs=(
            P(seq, None),
            P(seq, None),
            P(),
            P(),
            P(),
            P(seq, "head"),
            P(seq, "head"),
            P(seq, "head"),
            P(seq, "head"),
            P("head"),
            P(None, "head"),
            P(None, "head"),
            P(None, "head"),
            P(),
            P("head", seq),
            P(),
            P(seq, "head"),
            P(seq, "head"),
            P("head", seq),
        ),
        out_specs=(
            P(seq, None),
            P(seq, None),
            P(),
            P(seq, "head"),
            P(seq, "head"),
            P(seq, "head"),
            P(seq, "head"),
            P("head"),
            P(None, "head"),
            P(None, "head"),
            P(None, "head"),
            P(),
            P("head", seq),
            P(),
            P(seq, "head"),
            P(seq, "head"),
            P("head", seq),
        ),
        check_vma=False,
    )
```
